32 devices in a mesh: group: 8 (over z, core), lane: 4 (over y, x).
Axes of the slice: x: 2, y: 2, z: 4, core: 2. Of those that a mesh axis runs over, the one named last changes fastest.
Arguments:
- node_feat: float32 [16384, 128], P(('group', 'lane')), may hold values from -6 to 6
- hub_feat: float32 [128, 128], P('lane'), may hold values from -6 to 6
- edge_feat: float32 [65536, 128], P(('group', 'lane')), may hold values from -6 to 6
- src_slot: int32 [65536], P(('group', 'lane')), may hold values from 0 to 831, as said below
- dst_slot: int32 [65536], P(('group', 'lane')), may hold values from 0 to 831, as said below
- sign_bit: int32 [65536], P(('group', 'lane')), may hold values from 0 to 1
- send_rows: int32 [128, 48], P(('group', 'lane')), may hold values from -1 to 511, as said below
- w_edge_in: float32 [384, 512], replicated, may hold values from -0.3125 to 0.3125
- b_edge_in: float32 [512], replicated, may hold values from -3 to 3
- w_edge_out: float32 [512, 128], replicated, may hold values from -0.25 to 0.25
- b_edge_out: float32 [128], replicated, may hold values from -3 to 3
- w_node_in: float32 [256, 512], replicated, may hold values from -0.375 to 0.375
- b_node_in: float32 [512], replicated, may hold values from -3 to 3
- w_node_out: float32 [512, 128], replicated, may hold values from -0.25 to 0.25
- b_node_out: float32 [128], replicated, may hold values from -3 to 3
Outputs:
- node_out: float32 [16384, 128], P(('group', 'lane'))
- hub_out: float32 [128, 128], P('lane')
The draws below stay inside these ranges and needn't reach their ends.
Inputs may be any that keep to these rules, and one draw needn't show every extreme that they name: `send_rows`: row d * 4 + p lists local rows of device d's vertices mirrored on lane p of d's group: distinct rows, then -1 to the end. Lists hold 0 to 48 rows, and one list of every device holds 48. `src_slot`: mirror rows named by an edge are live: row 512 + p * 48 + c with c below the length of lane p's list to this device's lane. `dst_slot`: as for src_slot.
All inputs are finite; a program needn't handle non-finite values.
Results may differ from the reference program's by a relative error of at most 0.00005.
Values sent between devices are 32-bit elements; how exact they have to be, the bound alone decides.
A program may use at most 64 MiB of HBM per device.

```python
import jax
import jax.numpy as jnp
from jax import lax

D = 128
HID = 512
E_DEV = 2048
V_DEV = 512
CAP = 48
H = 128
V_ALL = 16384
E_ALL = 65536
LISTS = 128
N_LANE = 4


def mirror_counts(key):
    base = jax.random.fold_in(key, 101)
    first_key, second_key, pick_key = jax.random.split(base, 3)
    senders = LISTS // N_LANE
    first = jax.random.randint(first_key, (senders, N_LANE), 0, CAP + 1)
    second = jax.random.randint(second_key, (senders, N_LANE), 0, CAP + 1)
    counts = first * second // CAP
    full_lane = jax.random.randint(pick_key, (senders, 1), 0, N_LANE)
    lanes_row = jnp.arange(N_LANE, dtype=jnp.int32)[None, :]
    return jnp.where(lanes_row == full_lane, CAP, counts).astype(jnp.int32)


def edge_slots(key, counts):
    kind_key, lane_key, column_key, master_key, hub_key = jax.random.split(key, 5)
    device = jnp.arange(E_ALL, dtype=jnp.int32) // E_DEV
    group_of = device // N_LANE
    lane_of = device % N_LANE
    kind = jax.random.randint(kind_key, (E_ALL,), 0, 8)
    peer_lane = jax.random.randint(lane_key, (E_ALL,), 0, N_LANE)
    live_count = counts[group_of * N_LANE + peer_lane, lane_of]
    column = jax.random.randint(column_key, (E_ALL,), 0, CAP) % jnp.maximum(live_count, 1)
    master = jax.random.randint(master_key, (E_ALL,), 0, V_DEV)
    hub_index = jax.random.randint(hub_key, (E_ALL,), 0, H)
    use_mirror = (kind >= 4) & (kind < 7) & (live_count > 0)
    use_hub = kind == 7
    slot = jnp.where(use_hub, V_DEV + N_LANE * CAP + hub_index, jnp.where(use_mirror, V_DEV + peer_lane * CAP + column, master))
    return slot.astype(jnp.int32)


def draw_send_rows(key, part):
    counts = mirror_counts(key)
    key = jax.random.fold_in(key, 3)
    keys = jax.random.split(key, LISTS)
    chosen = jax.vmap(lambda single: jax.random.permutation(single, V_DEV)[:CAP])(keys)
    keep = jnp.arange(CAP, dtype=jnp.int32)[None, :] < counts.reshape(-1)[:, None]
    return jnp.where(keep, chosen, -1).astype(jnp.int32)


def draw_src_slot(key, part):
    counts = mirror_counts(key)
    key = jax.random.fold_in(key, 11)
    return edge_slots(key, counts)


def draw_dst_slot(key, part):
    counts = mirror_counts(key)
    key = jax.random.fold_in(key, 13)
    return edge_slots(key, counts)


def touch_ends(drawn, own_key, smallest, largest):
    spot = [jax.random.randint(jax.random.fold_in(own_key, axis), (), 0, length) for axis, length in enumerate(drawn.shape)]
    main_axis = drawn.shape.index(max(drawn.shape))
    next_to = spot[:main_axis] + [(spot[main_axis] + 1) % drawn.shape[main_axis]] + spot[main_axis + 1:]
    return drawn.at[tuple(spot)].set(smallest).at[tuple(next_to)].set(largest)


def block_scale(stream_key, extent, pieces, low, largest):
    def one(dim, blocks):
        draws = jax.random.uniform(jax.random.fold_in(jax.random.fold_in(stream_key, 6), dim), (blocks,), jnp.float32, low / len(pieces), largest / len(pieces))
        return jnp.repeat(jnp.exp(draws), extent[dim] // blocks).reshape((-1,) + (1,) * (len(extent) - dim - 1))

    gain = one(*pieces[0])
    for cut in pieces[1:]:
        gain = gain * one(*cut)
    return gain


def centred(rng, extent, scale, limit, shards=(), held_as=jnp.bfloat16):
    drawn = scale * jax.random.normal(rng, extent, jnp.float32)
    if shards:
        drawn = drawn * block_scale(rng, extent, shards, -0.22, 0.18)
    return jnp.clip(drawn, -limit, limit).astype(held_as)


def setup_inputs(seed: int = 0) -> dict:
    seeds = jax.random.split(jax.random.key(seed), 16)
    return {
        "node_feat": centred(seeds[0], (V_ALL, D), 1.0, 6.0, ((0, 32),), jnp.float32),
        "hub_feat": centred(seeds[1], (H, D), 1.0, 6.0, ((0, 4),), jnp.float32),
        "edge_feat": centred(seeds[2], (E_ALL, D), 1.0, 6.0, ((0, 32),), jnp.float32),
        "src_slot": draw_src_slot(jax.random.fold_in(seeds[15], 71), 0),
        "dst_slot": draw_dst_slot(jax.random.fold_in(seeds[15], 71), 0),
        "sign_bit": touch_ends(jax.random.randint(seeds[5], (E_ALL,), 0, 2), jax.random.fold_in(seeds[5], 1), 0, 1).astype(jnp.int32),
        "send_rows": draw_send_rows(jax.random.fold_in(seeds[15], 71), 0),
        "w_edge_in": centred(seeds[7], (3 * D, HID), (3 * D) ** -0.5, 0.3125, (), jnp.float32),
        "b_edge_in": centred(seeds[8], (HID,), 0.5, 3.0, (), jnp.float32),
        "w_edge_out": centred(seeds[9], (HID, D), HID ** -0.5, 0.25, (), jnp.float32),
        "b_edge_out": centred(seeds[10], (D,), 0.5, 3.0, (), jnp.float32),
        "w_node_in": centred(seeds[11], (2 * D, HID), (2 * D) ** -0.5, 0.375, (), jnp.float32),
        "b_node_in": centred(seeds[12], (HID,), 0.5, 3.0, (), jnp.float32),
        "w_node_out": centred(seeds[13], (HID, D), HID ** -0.5, 0.25, (), jnp.float32),
        "b_node_out": centred(seeds[14], (D,), 0.5, 3.0, (), jnp.float32),
    }


def product(left, right):
    return jnp.dot(left, right, precision=lax.Precision.HIGHEST, preferred_element_type=jnp.float32)


def resolve(slot, send_rows):
    device = jnp.arange(E_ALL, dtype=jnp.int32) // E_DEV
    group_of = device // N_LANE
    lane_of = device % N_LANE
    mirror_pos = jnp.clip(slot - V_DEV, 0, N_LANE * CAP - 1)
    peer_lane = mirror_pos // CAP
    column = mirror_pos % CAP
    sender = group_of * N_LANE + peer_lane
    list_row = send_rows[sender * N_LANE + lane_of, column]
    hub_index = jnp.clip(slot - V_DEV - N_LANE * CAP, 0, H - 1)
    mirrored = sender * V_DEV + jnp.maximum(list_row, 0)
    result = jnp.where(slot < V_DEV, device * V_DEV + slot,
                       jnp.where(slot < V_DEV + N_LANE * CAP, mirrored, V_ALL + hub_index))
    return result.astype(jnp.int32)


def reference(node_feat, hub_feat, edge_feat, src_slot, dst_slot, sign_bit, send_rows,
              w_edge_in, b_edge_in, w_edge_out, b_edge_out,
              w_node_in, b_node_in, w_node_out, b_node_out):
    features = jnp.concatenate([node_feat, hub_feat], 0)
    source_all = resolve(src_slot, send_rows)
    target_all = resolve(dst_slot, send_rows)
    block_count = E_ALL // E_DEV

    def edge_block(block):
        source, target, edge_rows, sign_code = block
        stacked = jnp.concatenate([features[source], features[target], edge_rows], 1)
        pre_act = product(stacked, w_edge_in) + b_edge_in
        message = product(jax.nn.silu(pre_act), w_edge_out) + b_edge_out
        return message * (2 * sign_code - 1).astype(jnp.float32)[:, None]

    messages = lax.map(edge_block, (source_all.reshape(block_count, E_DEV),
                                    target_all.reshape(block_count, E_DEV),
                                    edge_feat.reshape(block_count, E_DEV, D),
                                    sign_bit.reshape(block_count, E_DEV)))
    messages = messages.reshape(E_ALL, D)
    summed = jax.ops.segment_sum(messages, target_all, num_segments=V_ALL + H)
    degree = jax.ops.segment_sum(jnp.ones((E_ALL,), jnp.float32), target_all, num_segments=V_ALL + H)
    mean_message = summed / jnp.maximum(degree, 1.0)[:, None]
    hidden = jax.nn.silu(product(jnp.concatenate([features, mean_message], 1), w_node_in) + b_node_in)
    updated = features + product(hidden, w_node_out) + b_node_out
    return updated[:V_ALL], updated[V_ALL:]
```

```python
import functools
import math

import jax
import jax.numpy as jnp
from jax import lax
from jax.experimental import pallas as pl
from jax.experimental.pallas import tpu as pltpu
from jax.sharding import PartitionSpec as P

MESH = pl.DeviceIdType.MESH
F32, BF16 = jnp.float32, jnp.bfloat16


def split(x):
    hi = x.astype(BF16)
    return hi, (x - hi.astype(F32)).astype(BF16)


def dot(a, b):
    return jnp.dot(a, b, preferred_element_type=F32)


def silu(v):
    return v / (1.0 + jnp.exp(-v))


def column(row):
    return jnp.transpose(jnp.broadcast_to(row, (128, row.shape[1])))


def store_weights(w_ref, stack_ref, low_ref):
    for b in range(w_ref.shape[0] // 128):
        hi, lo = split(w_ref[128 * b : 128 * (b + 1), :])
        stack_ref[256 * b : 256 * b + 128, :] = hi
        stack_ref[256 * b + 128 : 256 * b + 256, :] = hi
        low_ref[128 * b : 128 * (b + 1), :] = lo


def store_out_weights(w_ref, pair_ref):
    hi, lo = split(w_ref[...])
    pair_ref[:, :128] = hi
    pair_ref[:, 128:] = lo


def out_layer(hidden, pair_ref):
    hi, lo = split(hidden)
    both = dot(hi, pair_ref[...])
    return both[:, :128] + both[:, 128:] + dot(lo, pair_ref[:, :128])


def kernel(
    sizes,
    node, hub, edge, src, dst, sgn, rows, w1, b1, w2, b2, w3, b3, w4, b4,
    node_out, hub_out,
    w1s, w1l, w2p, w3s, w3l, w4p,
    table, outbuf, mir, hubs, oh_s, oh_d, oh_t, sums, dacc, res, back, huba, hubb, hubsend,
    m_send, m_recv, h_send, h_recv, r_send, r_recv, a_send, a_recv, g_send, g_recv,
):
    L, G, V, CAP, H, HS, E, EB, T, TP = sizes
    LC = L * CAP
    lane = lax.axis_index("lane")
    group = lax.axis_index("group")
    barrier = pltpu.get_barrier_semaphore()
    lanes = [lax.rem(lane + k, L) for k in range(1, L)]
    groups = [lax.rem(group + k, G) for k in range(1, G)]
    for p in lanes:
        pl.semaphore_signal(barrier, inc=1, device_id=(group, p), device_id_type=MESH)
    for q in groups:
        pl.semaphore_signal(barrier, inc=1, device_id=(q, lane), device_id_type=MESH)

    hi, lo = split(node[...])
    table[:V, :128] = hi
    table[:V, 128:] = lo
    if TP > T:
        table[T:, :] = jnp.zeros((TP - T, 256), BF16)
    LCP = -(-LC // 128) * 128
    pieces = [rows[p : p + 1, :] for p in range(L)]
    if LCP > LC:
        pieces.append(jnp.full((1, LCP - LC), -1, jnp.int32))
    flat_rows = jnp.concatenate(pieces, axis=1)
    lane_iota = lax.broadcasted_iota(jnp.int32, (128, 128), 1)
    flat_col = column(flat_rows)[:LC]
    lane_iota_lc = lax.broadcasted_iota(jnp.int32, (LC, 128), 1)
    send_hot = jnp.concatenate(
        [jnp.where(flat_col == lane_iota_lc + 128 * k, 1.0, 0.0).astype(BF16) for k in range(V // 128)], axis=1
    )
    both = dot(send_hot, table[:V, :])
    outbuf[...] = both[:, :128] + both[:, 128:]

    pl.semaphore_wait(barrier, L - 1 + G - 1)

    def remote(src_ref, dst_ref, s_sem, r_sem, g, l):
        return pltpu.make_async_remote_copy(
            src_ref=src_ref, dst_ref=dst_ref, send_sem=s_sem, recv_sem=r_sem,
            device_id=(g, l), device_id_type=MESH,
        )

    def part(p, n, start=0):
        return pl.ds(pl.multiple_of(start + p * n, 16), n)

    sends = []
    for p in lanes:
        c = remote(outbuf.at[part(p, CAP)], mir.at[part(lane, CAP)], m_send.at[p], m_recv.at[lane], group, p)
        c.start()
        sends.append(c)
        c = remote(hub, hubs.at[part(lane, HS)], h_send.at[p], h_recv.at[lane], group, p)
        c.start()
        sends.append(c)
    mir[part(lane, CAP), :] = outbuf[part(lane, CAP), :]
    hubs[part(lane, HS), :] = hub[...]

    store_weights(w1, w1s, w1l)
    store_out_weights(w2, w2p)
    store_weights(w3, w3s, w3l)
    store_out_weights(w4, w4p)
    sums[...] = jnp.zeros(sums.shape, F32)
    dacc[...] = jnp.zeros(dacc.shape, F32)

    for p in lanes:
        remote(outbuf.at[part(p, CAP)], mir.at[part(p, CAP)], m_send.at[p], m_recv.at[p], group, p).wait_recv()
        remote(hub, hubs.at[part(p, HS)], h_send.at[p], h_recv.at[p], group, p).wait_recv()
    hi, lo = split(mir[...])
    table[V : V + LC, :128] = hi
    table[V : V + LC, 128:] = lo
    hi, lo = split(hubs[...])
    table[V + LC : T, :128] = hi
    table[V + LC : T, 128:] = lo

    NR = EB // 128
    sub_iota = lax.broadcasted_iota(jnp.int32, (T, 128), 0)

    def edge_block(i, carry):
        signs = []
        for j in range(NR):
            at = pl.ds(i * NR + j, 1)
            row = slice(128 * j, 128 * (j + 1))
            s_col = column(src[at, :])
            d_row = dst[at, :]
            d_col = column(d_row)
            for k in range(TP // 128):
                ids = lane_iota + 128 * k
                cols = slice(128 * k, 128 * (k + 1))
                oh_s[row, cols] = jnp.where(s_col == ids, 1.0, 0.0).astype(BF16)
                oh_d[row, cols] = jnp.where(d_col == ids, 1.0, 0.0).astype(BF16)
            hot = jnp.where(sub_iota == d_row, 1.0, 0.0)
            oh_t[:, row] = hot.astype(BF16)
            dacc[...] += hot
            signs.append((2 * column(sgn[at, :]) - 1).astype(F32))
        xs = dot(oh_s[...], table[...]).astype(BF16)
        xd = dot(oh_d[...], table[...]).astype(BF16)
        eh, el = split(edge[pl.ds(pl.multiple_of(i * EB, EB), EB), :])
        pre = dot(jnp.concatenate([xs, xd, eh, el], axis=1), w1s[...])
        pre = pre + dot(jnp.concatenate([xs[:, :128], xd[:, :128], eh], axis=1), w1l[...])
        h = silu(pre + b1[...])
        m = (out_layer(h, w2p) + b2[...]) * jnp.concatenate(signs, axis=0)
        mh, ml = split(m)
        sums[...] += dot(oh_t[...], jnp.concatenate([mh, ml], axis=1))
        return carry

    lax.fori_loop(0, E // EB, edge_block, 0)

    res[:, :128] = sums[:, :128] + sums[:, 128:]
    res[:, 128:] = dot(dacc[...].astype(BF16), jnp.ones((128, 128), BF16))
    for p in lanes:
        c = remote(res.at[part(p, HS, V + LC)], huba.at[part(lane, HS)], a_send.at[p], a_recv.at[lane], group, p)
        c.start()
        sends.append(c)
    for p in lanes:
        c = remote(res.at[part(p, CAP, V)], back.at[part(lane, CAP)], r_send.at[p], r_recv.at[lane], group, p)
        c.start()
        sends.append(c)
    huba[part(lane, HS), :] = res[part(lane, HS, V + LC), :]
    back[part(lane, CAP), :] = res[part(lane, CAP, V), :]

    for p in lanes:
        remote(res.at[part(p, HS)], huba.at[part(p, HS)], a_send.at[p], a_recv.at[p], group, p).wait_recv()
    total = huba[:HS, :]
    for p in range(1, L):
        total = total + huba[HS * p : HS * (p + 1), :]
    deg = jnp.concatenate([total[:, 128:], jnp.zeros((128 - HS, 128), F32)], axis=0)
    hubsend[:HS, :] = total[:, :128]
    hubsend[HS:, :] = jnp.transpose(deg)[:8, :]
    for q in groups:
        c = remote(hubsend, hubb.at[group], g_send.at[q], g_recv.at[group], q, lane)
        c.start()
        sends.append(c)
    hubb[group] = hubsend[...]

    for p in lanes:
        remote(res.at[part(p, CAP)], back.at[part(p, CAP)], r_send.at[p], r_recv.at[p], group, p).wait_recv()
    v_iota = lax.broadcasted_iota(jnp.int32, (V, LC), 0)
    back_hot = jnp.where(v_iota == flat_rows[:, :LC], 1.0, 0.0).astype(BF16)
    sh, sl = split(back[:, :128])
    dh, dl = split(back[:, 128:])
    got = dot(back_hot, jnp.concatenate([sh, sl], axis=1))
    got_deg = dot(back_hot, jnp.concatenate([dh, dl], axis=1))

    def update(x, summed, degree):
        xh, xl = split(x)
        mh, ml = split(summed / jnp.maximum(degree, 1.0))
        pre = dot(jnp.concatenate([xh, xl, mh, ml], axis=1), w3s[...])
        pre = pre + dot(jnp.concatenate([xh, mh], axis=1), w3l[...])
        return x + out_layer(silu(pre + b3[...]), w4p) + b4[...]

    node_out[...] = update(
        node[...],
        res[:V, :128] + got[:, :128] + got[:, 128:],
        res[:V, 128:] + got_deg[:, :128] + got_deg[:, 128:],
    )

    for q in groups:
        remote(hubsend, hubb.at[q], g_send.at[q], g_recv.at[q], q, lane).wait_recv()
    whole = hubb[0]
    for q in range(1, G):
        whole = whole + hubb[q]
    hub_out[...] = update(hub[...], whole[:HS, :], column(whole[HS : HS + 1, :])[:HS])
    for c in sends:
        c.wait_send()


def per_device(node, hub, edge, src, dst, sgn, rows, w1, b1, w2, b2, w3, b3, w4, b4):
    L, G = lax.axis_size("lane"), lax.axis_size("group")
    V, D = node.shape
    CAP = rows.shape[1]
    HS = hub.shape[0]
    H = HS * L
    E = edge.shape[0]
    HID = w1.shape[1]
    EB = math.gcd(512, E)
    T = V + L * CAP + H
    TP = -(-T // 128) * 128
    sizes = (L, G, V, CAP, H, HS, E, EB, T, TP)
    dma = pltpu.SemaphoreType.DMA
    vmem = pl.BlockSpec(memory_space=pltpu.VMEM)
    return pl.pallas_call(
        functools.partial(kernel, sizes),
        out_shape=(jax.ShapeDtypeStruct((V, D), F32), jax.ShapeDtypeStruct((HS, D), F32)),
        in_specs=[vmem] * 15,
        out_specs=(vmem, vmem),
        scratch_shapes=[
            pltpu.VMEM((6 * D, HID), BF16),
            pltpu.VMEM((3 * D, HID), BF16),
            pltpu.VMEM((HID, 2 * D), BF16),
            pltpu.VMEM((4 * D, HID), BF16),
            pltpu.VMEM((2 * D, HID), BF16),
            pltpu.VMEM((HID, 2 * D), BF16),
            pltpu.VMEM((TP, 2 * D), BF16),
            pltpu.VMEM((L * CAP, D), F32),
            pltpu.VMEM((L * CAP, D), F32),
            pltpu.VMEM((H, D), F32),
            pltpu.VMEM((EB, TP), BF16),
            pltpu.VMEM((EB, TP), BF16),
            pltpu.VMEM((T, EB), BF16),
            pltpu.VMEM((T, 2 * D), F32),
            pltpu.VMEM((T, 128), F32),
            pltpu.VMEM((T, 2 * D), F32),
            pltpu.VMEM((L * CAP, 2 * D), F32),
            pltpu.VMEM((H, 2 * D), F32),
            pltpu.VMEM((G, HS + 8, D), F32),
            pltpu.VMEM((HS + 8, D), F32),
        ]
        + [dma((L,))] * 8
        + [dma((G,))] * 2,
        compiler_params=pltpu.CompilerParams(
            collective_id=0, has_side_effects=True, vmem_limit_bytes=48 * 2**20
        ),
    )(
        node, hub, edge, src.reshape(-1, 128), dst.reshape(-1, 128), sgn.reshape(-1, 128), rows,
        w1, b1.reshape(1, -1), w2, b2.reshape(1, -1), w3, b3.reshape(1, -1), w4, b4.reshape(1, -1),
    )


def solution(mesh):
    rows = P(("group", "lane"), None)
    flat = P(("group", "lane"))
    return jax.shard_map(
        per_device,
        mesh=mesh,
        in_specs=(rows, P("lane", None), rows, flat, flat, flat, rows) + (P(),) * 8,
        out_specs=(rows, P("lane", None)),
        check_vma=False,
    )
```

```python
import functools
import math

import jax
import jax.numpy as jnp
from jax import lax
from jax.experimental import pallas as pl
from jax.experimental.pallas import tpu as pltpu
from jax.sharding import PartitionSpec as P

MESH = pl.DeviceIdType.MESH
F32, BF16 = jnp.float32, jnp.bfloat16


def split(x):
    hi = x.astype(BF16)
    return hi, (x - hi.astype(F32)).astype(BF16)


def dot(a, b):
    return jnp.dot(a, b, preferred_element_type=F32)


def silu(v):
    return v + v * jnp.tanh(v)


def column(row):
    return jnp.transpose(jnp.broadcast_to(row, (128, row.shape[1])))


def store_weights(w_ref, stack_ref, low_ref):
    for b in range(w_ref.shape[0] // 128):
        hi, lo = split(0.5 * w_ref[128 * b : 128 * (b + 1), :])
        stack_ref[256 * b : 256 * b + 128, :] = hi
        stack_ref[256 * b + 128 : 256 * b + 256, :] = hi
        low_ref[128 * b : 128 * (b + 1), :] = lo


def store_out_weights(w_ref, pair_ref):
    hi, lo = split(w_ref[...])
    pair_ref[:, :128] = hi
    pair_ref[:, 128:] = lo


def out_layer(hidden, pair_ref):
    hi, lo = split(hidden)
    both = dot(hi, pair_ref[...])
    return both[:, :128] + both[:, 128:] + dot(lo, pair_ref[:, :128])


def kernel(
    sizes,
    node_h, hub_h, edge_h, src_h, dst_h, sgn_h, rows_h, w1_h, b1_h, w2_h, b2_h, w3_h, b3_h, w4_h, b4_h,
    node_out, hub_out,
    node, hub, edge, src, dst, sgn, rows, w1, b1, w2, b2, w3, b3, w4, b4, in_sem,
    w1s, w1l, w2p, w3s, w3l, w4p,
    table, outbuf, mir, hubs, oh_s, oh_d, oh_t, sums, dacc, res, back, huba, hubb, hubsend,
    m_send, m_recv, h_send, h_recv, r_send, r_recv, a_send, a_recv, g_send, g_recv,
):
    L, G, V, CAP, H, HS, E, EB, T, TP = sizes
    LC = L * CAP
    lane = lax.axis_index("lane")
    group = lax.axis_index("group")
    barrier = pltpu.get_barrier_semaphore()
    lanes = [lax.rem(lane + k, L) for k in range(1, L)]
    groups = [lax.rem(group + k, G) for k in range(1, G)]
    for p in lanes:
        pl.semaphore_signal(barrier, inc=1, device_id=(group, p), device_id_type=MESH)
    for q in groups:
        pl.semaphore_signal(barrier, inc=1, device_id=(q, lane), device_id_type=MESH)

    far = (rows_h, node_h, hub_h, src_h, dst_h, w1_h, edge_h, w2_h, sgn_h, b1_h, b2_h, w3_h, w4_h, b3_h, b4_h)
    near = (rows, node, hub, src, dst, w1, edge, w2, sgn, b1, b2, w3, w4, b3, b4)
    loads = [pltpu.make_async_copy(f, n, in_sem.at[i]) for i, (f, n) in enumerate(zip(far, near))]
    for c in loads:
        c.start()
    for c in loads[:3]:
        c.wait()

    hi, lo = split(node[...])
    table[:V, :128] = hi
    table[:V, 128:] = lo
    if TP > T:
        table[T:, :] = jnp.zeros((TP - T, 256), BF16)
    LCP = -(-LC // 128) * 128
    pieces = [rows[p : p + 1, :] for p in range(L)]
    if LCP > LC:
        pieces.append(jnp.full((1, LCP - LC), -1, jnp.int32))
    flat_rows = jnp.concatenate(pieces, axis=1)
    lane_iota = lax.broadcasted_iota(jnp.int32, (128, 128), 1)
    flat_col = column(flat_rows)[:LC]
    lane_iota_lc = lax.broadcasted_iota(jnp.int32, (LC, 128), 1)
    send_hot = jnp.concatenate(
        [jnp.where(flat_col == lane_iota_lc + 128 * k, 1.0, 0.0).astype(BF16) for k in range(V // 128)], axis=1
    )
    both = dot(send_hot, table[:V, :])
    outbuf[...] = both[:, :128] + both[:, 128:]

    pl.semaphore_wait(barrier, L - 1 + G - 1)

    def remote(src_ref, dst_ref, s_sem, r_sem, g, l):
        return pltpu.make_async_remote_copy(
            src_ref=src_ref, dst_ref=dst_ref, send_sem=s_sem, recv_sem=r_sem,
            device_id=(g, l), device_id_type=MESH,
        )

    def part(p, n, start=0):
        return pl.ds(pl.multiple_of(start + p * n, 16), n)

    sends = []
    for p in lanes:
        c = remote(outbuf.at[part(p, CAP)], mir.at[part(lane, CAP)], m_send.at[p], m_recv.at[lane], group, p)
        c.start()
        sends.append(c)
        c = remote(hub, hubs.at[part(lane, HS)], h_send.at[p], h_recv.at[lane], group, p)
        c.start()
        sends.append(c)
    mir[part(lane, CAP), :] = outbuf[part(lane, CAP), :]
    hubs[part(lane, HS), :] = hub[...]

    for c in loads[3:]:
        c.wait()
    store_weights(w1, w1s, w1l)
    store_out_weights(w2, w2p)
    store_weights(w3, w3s, w3l)
    store_out_weights(w4, w4p)
    sums[...] = jnp.zeros(sums.shape, F32)
    dacc[...] = jnp.zeros(dacc.shape, BF16)

    for p in lanes:
        remote(outbuf.at[part(p, CAP)], mir.at[part(p, CAP)], m_send.at[p], m_recv.at[p], group, p).wait_recv()
        remote(hub, hubs.at[part(p, HS)], h_send.at[p], h_recv.at[p], group, p).wait_recv()
    hi, lo = split(mir[...])
    table[V : V + LC, :128] = hi
    table[V : V + LC, 128:] = lo
    hi, lo = split(hubs[...])
    table[V + LC : T, :128] = hi
    table[V + LC : T, 128:] = lo

    NR = EB // 128
    lane_id = lane_iota.astype(F32).astype(BF16)
    sub_id = lax.broadcasted_iota(jnp.int32, (128, 128), 0).astype(F32).astype(BF16)
    one, zero = jnp.ones((128, 128), BF16), jnp.zeros((128, 128), BF16)

    def digits(ids):
        high = ids >> 7
        return (ids & 127).astype(F32).astype(BF16), high.astype(F32).astype(BF16)

    def edge_block(i, carry):
        signs = []
        for j in range(NR):
            at = pl.ds(i * NR + j, 1)
            row = slice(128 * j, 128 * (j + 1))
            d_row = dst[at, :]
            s_low, s_high = digits(column(src[at, :]))
            d_low, d_high = digits(column(d_row))
            r_low, r_high = digits(jnp.broadcast_to(d_row, (128, 128)))
            s_hot = jnp.where(s_low == lane_id, one, zero)
            d_hot = jnp.where(d_low == lane_id, one, zero)
            r_hot = jnp.where(r_low == sub_id, one, zero)
            for k in range(TP // 128):
                cols = slice(128 * k, 128 * (k + 1))
                k16 = jnp.asarray(k, BF16)
                oh_s[row, cols] = jnp.where(s_high == k16, s_hot, zero)
                oh_d[row, cols] = jnp.where(d_high == k16, d_hot, zero)
                n = min(128, T - 128 * k)
                hot = jnp.where(r_high == k16, r_hot, zero)[:n]
                oh_t[128 * k : 128 * k + n, row] = hot
                dacc[128 * k : 128 * k + n, :] += hot
            signs.append((2 * column(sgn[at, :]) - 1).astype(F32))
        xs = dot(oh_s[...], table[...]).astype(BF16)
        xd = dot(oh_d[...], table[...]).astype(BF16)
        eh, el = split(edge[pl.ds(pl.multiple_of(i * EB, EB), EB), :])
        pre = dot(jnp.concatenate([xs, xd, eh, el], axis=1), w1s[...])
        pre = pre + dot(jnp.concatenate([xs[:, :128], xd[:, :128], eh], axis=1), w1l[...])
        h = silu(pre + 0.5 * b1[...])
        m = (out_layer(h, w2p) + b2[...]) * jnp.concatenate(signs, axis=0)
        mh, ml = split(m)
        sums[...] += dot(oh_t[...], jnp.concatenate([mh, ml], axis=1))
        return carry

    lax.fori_loop(0, E // EB, edge_block, 0)

    res[:, :128] = sums[:, :128] + sums[:, 128:]
    res[:, 128:] = dot(dacc[...], jnp.ones((128, 128), BF16))
    for p in lanes:
        c = remote(res.at[part(p, HS, V + LC)], huba.at[part(lane, HS)], a_send.at[p], a_recv.at[lane], group, p)
        c.start()
        sends.append(c)
    for p in lanes:
        c = remote(res.at[part(p, CAP, V)], back.at[part(lane, CAP)], r_send.at[p], r_recv.at[lane], group, p)
        c.start()
        sends.append(c)
    huba[part(lane, HS), :] = res[part(lane, HS, V + LC), :]
    back[part(lane, CAP), :] = res[part(lane, CAP, V), :]

    for p in lanes:
        remote(res.at[part(p, HS)], huba.at[part(p, HS)], a_send.at[p], a_recv.at[p], group, p).wait_recv()
    total = huba[:HS, :]
    for p in range(1, L):
        total = total + huba[HS * p : HS * (p + 1), :]
    deg = jnp.concatenate([total[:, 128:], jnp.zeros((128 - HS, 128), F32)], axis=0)
    hubsend[:HS, :] = total[:, :128]
    hubsend[HS:, :] = jnp.transpose(deg)[:8, :]
    for q in groups:
        c = remote(hubsend, hubb.at[group], g_send.at[q], g_recv.at[group], q, lane)
        c.start()
        sends.append(c)
    hubb[group] = hubsend[...]

    for p in lanes:
        remote(res.at[part(p, CAP)], back.at[part(p, CAP)], r_send.at[p], r_recv.at[p], group, p).wait_recv()
    v_iota = lax.broadcasted_iota(jnp.int32, (V, LC), 0)
    back_hot = jnp.where(v_iota == flat_rows[:, :LC], 1.0, 0.0).astype(BF16)
    sh, sl = split(back[:, :128])
    dh, dl = split(back[:, 128:])
    got = dot(back_hot, jnp.concatenate([sh, sl], axis=1))
    got_deg = dot(back_hot, jnp.concatenate([dh, dl], axis=1))

    def update(x, summed, degree):
        xh, xl = split(x)
        mh, ml = split(summed / jnp.maximum(degree, 1.0))
        pre = dot(jnp.concatenate([xh, xl, mh, ml], axis=1), w3s[...])
        pre = pre + dot(jnp.concatenate([xh, mh], axis=1), w3l[...])
        return x + out_layer(silu(pre + 0.5 * b3[...]), w4p) + b4[...]

    node_out[...] = update(
        node[...],
        res[:V, :128] + got[:, :128] + got[:, 128:],
        res[:V, 128:] + got_deg[:, :128] + got_deg[:, 128:],
    )

    for q in groups:
        remote(hubsend, hubb.at[q], g_send.at[q], g_recv.at[q], q, lane).wait_recv()
    whole = hubb[0]
    for q in range(1, G):
        whole = whole + hubb[q]
    hub_out[...] = update(hub[...], whole[:HS, :], column(whole[HS : HS + 1, :])[:HS])
    for c in sends:
        c.wait_send()


def per_device(node, hub, edge, src, dst, sgn, rows, w1, b1, w2, b2, w3, b3, w4, b4):
    L, G = lax.axis_size("lane"), lax.axis_size("group")
    V, D = node.shape
    CAP = rows.shape[1]
    HS = hub.shape[0]
    H = HS * L
    E = edge.shape[0]
    HID = w1.shape[1]
    EB = math.gcd(512, E)
    T = V + L * CAP + H
    TP = -(-T // 128) * 128
    sizes = (L, G, V, CAP, H, HS, E, EB, T, TP)
    assert E <= 256 * 128
    dma = pltpu.SemaphoreType.DMA
    vmem = pl.BlockSpec(memory_space=pltpu.VMEM)
    args = (
        node, hub, edge, src.reshape(-1, 128), dst.reshape(-1, 128), sgn.reshape(-1, 128), rows,
        w1, b1.reshape(1, -1), w2, b2.reshape(1, -1), w3, b3.reshape(1, -1), w4, b4.reshape(1, -1),
    )
    return pl.pallas_call(
        functools.partial(kernel, sizes),
        out_shape=(jax.ShapeDtypeStruct((V, D), F32), jax.ShapeDtypeStruct((HS, D), F32)),
        in_specs=[pl.BlockSpec(memory_space=pltpu.HBM)] * 15,
        out_specs=(vmem, vmem),
        scratch_shapes=[pltpu.VMEM(a.shape, a.dtype) for a in args]
        + [dma((15,))]
        + [
            pltpu.VMEM((6 * D, HID), BF16),
            pltpu.VMEM((3 * D, HID), BF16),
            pltpu.VMEM((HID, 2 * D), BF16),
            pltpu.VMEM((4 * D, HID), BF16),
            pltpu.VMEM((2 * D, HID), BF16),
            pltpu.VMEM((HID, 2 * D), BF16),
            pltpu.VMEM((TP, 2 * D), BF16),
            pltpu.VMEM((L * CAP, D), F32),
            pltpu.VMEM((L * CAP, D), F32),
            pltpu.VMEM((H, D), F32),
            pltpu.VMEM((EB, TP), BF16),
            pltpu.VMEM((EB, TP), BF16),
            pltpu.VMEM((T, EB), BF16),
            pltpu.VMEM((T, 2 * D), F32),
            pltpu.VMEM((T, 128), BF16),
            pltpu.VMEM((T, 2 * D), F32),
            pltpu.VMEM((L * CAP, 2 * D), F32),
            pltpu.VMEM((H, 2 * D), F32),
            pltpu.VMEM((G, HS + 8, D), F32),
            pltpu.VMEM((HS + 8, D), F32),
        ]
        + [dma((L,))] * 8
        + [dma((G,))] * 2,
        compiler_params=pltpu.CompilerParams(
            collective_id=0, has_side_effects=True, vmem_limit_bytes=64 * 2**20
        ),
    )(*args)


def solution(mesh):
    rows = P(("group", "lane"), None)
    flat = P(("group", "lane"))
    return jax.shard_map(
        per_device,
        mesh=mesh,
        in_specs=(rows, P("lane", None), rows, flat, flat, flat, rows) + (P(),) * 8,
        out_specs=(rows, P("lane", None)),
        check_vma=False,
    )
```

```python
import functools
import math

import jax
import jax.numpy as jnp
from jax import lax
from jax.experimental import pallas as pl
from jax.experimental.pallas import tpu as pltpu
from jax.sharding import PartitionSpec as P

MESH = pl.DeviceIdType.MESH
F32, BF16 = jnp.float32, jnp.bfloat16


def split(x):
    hi = x.astype(BF16)
    return hi, (x - hi.astype(F32)).astype(BF16)


def dot(a, b):
    return jnp.dot(a, b, preferred_element_type=F32)


def silu(v):
    return v + v * jnp.tanh(v)


def column(row):
    return jnp.transpose(jnp.broadcast_to(row, (128, row.shape[1])))


def store_weights(w_ref, stack_ref, low_ref):
    for b in range(w_ref.shape[0] // 128):
        hi, lo = split(0.5 * w_ref[128 * b : 128 * (b + 1), :])
        stack_ref[256 * b : 256 * b + 128, :] = hi
        stack_ref[256 * b + 128 : 256 * b + 256, :] = hi
        low_ref[128 * b : 128 * (b + 1), :] = lo


def store_out_weights(w_ref, pair_ref):
    hi, lo = split(w_ref[...])
    pair_ref[:, :128] = hi
    pair_ref[:, 128:] = lo


def out_layer(hidden, pair_ref):
    hi, lo = split(hidden)
    both = dot(hi, pair_ref[...])
    return both[:, :128] + both[:, 128:] + dot(lo, pair_ref[:, :128])


def kernel(
    sizes,
    node_h, hub_h, edge_h, src_h, dst_h, sgn_h, rows_h, w1_h, b1_h, w2_h, b2_h, w3_h, b3_h, w4_h, b4_h,
    node_out, hub_out,
    node, hub, edge, src, dst, sgn, rows, w1, b1, w2, b2, w3, b3, w4, b4, in_sem,
    w1s, w1l, w2p, w3s, w3l, w4p,
    table, outbuf, mir, hubs, own_s, own_d, oh_s, oh_d, x_s, x_d, oh_t, sums, dacc, msg, got_msg, hubb, hubsend,
    m_send, m_recv, h_send, h_recv, r_send, r_recv, a_send, a_recv, g_send, g_recv,
):
    L, G, V, CAP, H, HS, E, EB, T, TP = sizes
    LC = L * CAP
    lane = lax.axis_index("lane")
    group = lax.axis_index("group")
    barrier = pltpu.get_barrier_semaphore()
    lanes = [lax.rem(lane + k, L) for k in range(1, L)]
    groups = [lax.rem(group + k, G) for k in range(1, G)]
    for p in lanes:
        pl.semaphore_signal(barrier, inc=1, device_id=(group, p), device_id_type=MESH)
    for q in groups:
        pl.semaphore_signal(barrier, inc=1, device_id=(q, lane), device_id_type=MESH)

    far = (rows_h, node_h, hub_h, src_h, dst_h, w1_h, edge_h, w2_h, sgn_h, b1_h, b2_h, w3_h, w4_h, b3_h, b4_h)
    near = (rows, node, hub, src, dst, w1, edge, w2, sgn, b1, b2, w3, w4, b3, b4)
    loads = [pltpu.make_async_copy(f, n, in_sem.at[i]) for i, (f, n) in enumerate(zip(far, near))]
    for c in loads:
        c.start()
    for c in loads[:3]:
        c.wait()

    hi, lo = split(node[...])
    table[:V, :128] = hi
    table[:V, 128:] = lo
    if TP > T:
        table[T:, :] = jnp.zeros((TP - T, 256), BF16)
    LCP = -(-LC // 128) * 128
    pieces = [rows[p : p + 1, :] for p in range(L)]
    if LCP > LC:
        pieces.append(jnp.full((1, LCP - LC), -1, jnp.int32))
    flat_rows = jnp.concatenate(pieces, axis=1)
    lane_iota = lax.broadcasted_iota(jnp.int32, (128, 128), 1)
    flat_col = column(flat_rows)[:LC]
    lane_iota_lc = lax.broadcasted_iota(jnp.int32, (LC, 128), 1)
    send_hot = jnp.concatenate(
        [jnp.where(flat_col == lane_iota_lc + 128 * k, 1.0, 0.0).astype(BF16) for k in range(V // 128)], axis=1
    )
    both = dot(send_hot, table[:V, :])
    outbuf[...] = both[:, :128] + both[:, 128:]

    pl.semaphore_wait(barrier, L - 1 + G - 1)

    def remote(src_ref, dst_ref, s_sem, r_sem, g, l):
        return pltpu.make_async_remote_copy(
            src_ref=src_ref, dst_ref=dst_ref, send_sem=s_sem, recv_sem=r_sem,
            device_id=(g, l), device_id_type=MESH,
        )

    def part(p, n, start=0):
        return pl.ds(pl.multiple_of(start + p * n, 16), n)

    sends = []
    for p in lanes:
        c = remote(outbuf.at[part(p, CAP)], mir.at[part(lane, CAP)], m_send.at[p], m_recv.at[lane], group, p)
        c.start()
        sends.append(c)
        c = remote(hub, hubs.at[part(lane, HS)], h_send.at[p], h_recv.at[lane], group, p)
        c.start()
        sends.append(c)
    mir[part(lane, CAP), :] = outbuf[part(lane, CAP), :]
    hubs[part(lane, HS), :] = hub[...]

    for c in loads[3:5]:
        c.wait()
    NR = EB // 128
    lane_id = lane_iota.astype(F32).astype(BF16)
    sub_id = lax.broadcasted_iota(jnp.int32, (128, 128), 0).astype(F32).astype(BF16)
    one, zero = jnp.ones((128, 128), BF16), jnp.zeros((128, 128), BF16)

    def digits(ids):
        high = ids >> 7
        return (ids & 127).astype(F32).astype(BF16), high.astype(F32).astype(BF16)

    def own_block(i, carry):
        for ids, own, other, found in ((src, own_s, oh_s, x_s), (dst, own_d, oh_d, x_d)):
            for j in range(NR):
                low, high = digits(column(ids[pl.ds(i * NR + j, 1), :]))
                hot = jnp.where(low == lane_id, one, zero)
                for k in range(TP // 128):
                    place = jnp.where(high == jnp.asarray(k, BF16), hot, zero)
                    if 128 * k < V:
                        own[128 * j : 128 * (j + 1), 128 * k : 128 * (k + 1)] = place
                    else:
                        other[part(i * NR + j, 128), 128 * k - V : 128 * (k + 1) - V] = place
            found[part(i, EB), :] = dot(own[...], table[:V, :]).astype(BF16)
        return carry

    lax.fori_loop(0, E // EB, own_block, 0)

    for c in loads[5:]:
        c.wait()
    store_weights(w1, w1s, w1l)
    store_out_weights(w2, w2p)
    store_weights(w3, w3s, w3l)
    store_out_weights(w4, w4p)
    sums[...] = jnp.zeros(sums.shape, F32)
    dacc[...] = jnp.zeros(dacc.shape, BF16)

    for p in lanes:
        remote(outbuf.at[part(p, CAP)], mir.at[part(p, CAP)], m_send.at[p], m_recv.at[p], group, p).wait_recv()
        remote(hub, hubs.at[part(p, HS)], h_send.at[p], h_recv.at[p], group, p).wait_recv()
    hi, lo = split(mir[...])
    table[V : V + LC, :128] = hi
    table[V : V + LC, 128:] = lo
    hi, lo = split(hubs[...])
    table[V + LC : T, :128] = hi
    table[V + LC : T, 128:] = lo

    def edge_block(i, carry):
        signs = []
        for j in range(NR):
            at = pl.ds(i * NR + j, 1)
            row = slice(128 * j, 128 * (j + 1))
            r_low, r_high = digits(jnp.broadcast_to(dst[at, :], (128, 128)))
            r_hot = jnp.where(r_low == sub_id, one, zero)
            for k in range(TP // 128):
                n = min(128, T - 128 * k)
                hot = jnp.where(r_high == jnp.asarray(k, BF16), r_hot, zero)[:n]
                oh_t[128 * k : 128 * k + n, row] = hot
                dacc[128 * k : 128 * k + n, :] += hot
            signs.append((2 * column(sgn[at, :]) - 1).astype(F32))
        here = part(i, EB)
        xs = (x_s[here, :].astype(F32) + dot(oh_s[here, :], table[V:, :])).astype(BF16)
        xd = (x_d[here, :].astype(F32) + dot(oh_d[here, :], table[V:, :])).astype(BF16)
        eh, el = split(edge[pl.ds(pl.multiple_of(i * EB, EB), EB), :])
        pre = dot(jnp.concatenate([xs, xd, eh, el], axis=1), w1s[...])
        pre = pre + dot(jnp.concatenate([xs[:, :128], xd[:, :128], eh], axis=1), w1l[...])
        h = silu(pre + 0.5 * b1[...])
        m = (out_layer(h, w2p) + b2[...]) * jnp.concatenate(signs, axis=0)
        mh, ml = split(m)
        sums[...] += dot(oh_t[...], jnp.concatenate([mh, ml], axis=1))
        return carry

    lax.fori_loop(0, E // EB, edge_block, 0)

    for p in range(L):
        hub_at, mir_at = V + LC + p * HS, V + p * CAP
        msg[p, :HS] = sums[hub_at : hub_at + HS, :128] + sums[hub_at : hub_at + HS, 128:]
        counts = jnp.concatenate(
            [dacc[hub_at : hub_at + HS, :], dacc[mir_at : mir_at + CAP, :], zero[: 128 - HS - CAP]], axis=0
        )
        msg[p, HS : HS + 8] = lax.dot_general(
            one[:8], counts, (((1,), (1,)), ((), ())), preferred_element_type=F32
        )
        msg[p, HS + 8 :] = sums[mir_at : mir_at + CAP, :128] + sums[mir_at : mir_at + CAP, 128:]
    first, second = pl.ds(0, HS + 8), pl.ds(HS + 8, CAP)
    for p in lanes:
        c = remote(msg.at[p, first], got_msg.at[lane, first], a_send.at[p], a_recv.at[lane], group, p)
        c.start()
        sends.append(c)
    for p in lanes:
        c = remote(msg.at[p, second], got_msg.at[lane, second], r_send.at[p], r_recv.at[lane], group, p)
        c.start()
        sends.append(c)
    got_msg[lane] = msg[lane]

    def own_part(x):
        return dot(jnp.concatenate(split(x), axis=1), w3s[:256]) + dot(x.astype(BF16), w3l[:128]) + 0.5 * b3[...]

    node_pre = own_part(node[...])
    hub_pre = own_part(hub[...])
    own_sum = sums[:V, :128] + sums[:V, 128:]
    own_deg = dot(dacc[:V, :], one)
    v_iota = lax.broadcasted_iota(jnp.int32, (V, LC), 0)
    back_hot = jnp.where(v_iota == flat_rows[:, :LC], 1.0, 0.0).astype(BF16)

    for p in lanes:
        remote(msg.at[p, first], got_msg.at[p, first], a_send.at[p], a_recv.at[p], group, p).wait_recv()
    total = got_msg[0, : HS + 8]
    for p in range(1, L):
        total = total + got_msg[p, : HS + 8]
    hubsend[...] = total
    for q in groups:
        c = remote(hubsend, hubb.at[group], g_send.at[q], g_recv.at[group], q, lane)
        c.start()
        sends.append(c)
    hubb[group] = hubsend[...]

    for p in lanes:
        remote(msg.at[p, second], got_msg.at[p, second], r_send.at[p], r_recv.at[p], group, p).wait_recv()
    sh, sl = split(jnp.concatenate([got_msg[p, HS + 8 :] for p in range(L)], axis=0))
    dh, dl = split(
        jnp.concatenate([column(got_msg[p, HS : HS + 1])[HS : HS + CAP] for p in range(L)], axis=0)
    )
    got = dot(back_hot, jnp.concatenate([sh, sl], axis=1))
    got_deg = dot(back_hot, jnp.concatenate([dh, dl], axis=1))

    def update(x, pre, summed, degree):
        mh, ml = split(summed / jnp.maximum(degree, 1.0))
        pre = pre + dot(jnp.concatenate([mh, ml], axis=1), w3s[256:]) + dot(mh, w3l[128:])
        return x + out_layer(silu(pre), w4p) + b4[...]

    node_out[...] = update(
        node[...],
        node_pre,
        own_sum + got[:, :128] + got[:, 128:],
        own_deg + got_deg[:, :128] + got_deg[:, 128:],
    )

    for q in groups:
        remote(hubsend, hubb.at[q], g_send.at[q], g_recv.at[q], q, lane).wait_recv()
    whole = hubb[0]
    for q in range(1, G):
        whole = whole + hubb[q]
    hub_out[...] = update(hub[...], hub_pre, whole[:HS, :], column(whole[HS : HS + 1, :])[:HS])
    for c in sends:
        c.wait_send()


def per_device(node, hub, edge, src, dst, sgn, rows, w1, b1, w2, b2, w3, b3, w4, b4):
    L, G = lax.axis_size("lane"), lax.axis_size("group")
    V, D = node.shape
    CAP = rows.shape[1]
    HS = hub.shape[0]
    H = HS * L
    E = edge.shape[0]
    HID = w1.shape[1]
    EB = math.gcd(512, E)
    T = V + L * CAP + H
    TP = -(-T // 128) * 128
    sizes = (L, G, V, CAP, H, HS, E, EB, T, TP)
    assert E <= 256 * 128 and HS + CAP <= 128 and V % 128 == 0
    dma = pltpu.SemaphoreType.DMA
    vmem = pl.BlockSpec(memory_space=pltpu.VMEM)
    args = (
        node, hub, edge, src.reshape(-1, 128), dst.reshape(-1, 128), sgn.reshape(-1, 128), rows,
        w1, b1.reshape(1, -1), w2, b2.reshape(1, -1), w3, b3.reshape(1, -1), w4, b4.reshape(1, -1),
    )
    return pl.pallas_call(
        functools.partial(kernel, sizes),
        out_shape=(jax.ShapeDtypeStruct((V, D), F32), jax.ShapeDtypeStruct((HS, D), F32)),
        in_specs=[pl.BlockSpec(memory_space=pltpu.HBM)] * 15,
        out_specs=(vmem, vmem),
        scratch_shapes=[pltpu.VMEM(a.shape, a.dtype) for a in args]
        + [dma((15,))]
        + [
            pltpu.VMEM((6 * D, HID), BF16),
            pltpu.VMEM((3 * D, HID), BF16),
            pltpu.VMEM((HID, 2 * D), BF16),
            pltpu.VMEM((4 * D, HID), BF16),
            pltpu.VMEM((2 * D, HID), BF16),
            pltpu.VMEM((HID, 2 * D), BF16),
            pltpu.VMEM((TP, 2 * D), BF16),
            pltpu.VMEM((L * CAP, D), F32),
            pltpu.VMEM((L * CAP, D), F32),
            pltpu.VMEM((H, D), F32),
            pltpu.VMEM((EB, V), BF16),
            pltpu.VMEM((EB, V), BF16),
            pltpu.VMEM((E, TP - V), BF16),
            pltpu.VMEM((E, TP - V), BF16),
            pltpu.VMEM((E, 2 * D), BF16),
            pltpu.VMEM((E, 2 * D), BF16),
            pltpu.VMEM((T, EB), BF16),
            pltpu.VMEM((T, 2 * D), F32),
            pltpu.VMEM((T, 128), BF16),
            pltpu.VMEM((L, HS + 8 + CAP, D), F32),
            pltpu.VMEM((L, HS + 8 + CAP, D), F32),
            pltpu.VMEM((G, HS + 8, D), F32),
            pltpu.VMEM((HS + 8, D), F32),
        ]
        + [dma((L,))] * 8
        + [dma((G,))] * 2,
        compiler_params=pltpu.CompilerParams(
            collective_id=0, has_side_effects=True, vmem_limit_bytes=64 * 2**20
        ),
    )(*args)


def solution(mesh):
    rows = P(("group", "lane"), None)
    flat = P(("group", "lane"))
    return jax.shard_map(
        per_device,
        mesh=mesh,
        in_specs=(rows, P("lane", None), rows, flat, flat, flat, rows) + (P(),) * 8,
        out_specs=(rows, P("lane", None)),
        check_vma=False,
    )
```

```python
import functools
import math

import jax
import jax.numpy as jnp
from jax import lax
from jax.experimental import pallas as pl
from jax.experimental.pallas import tpu as pltpu
from jax.sharding import PartitionSpec as P

MESH = pl.DeviceIdType.MESH
F32, BF16 = jnp.float32, jnp.bfloat16


def split(x):
    hi = x.astype(BF16)
    return hi, (x - hi.astype(F32)).astype(BF16)


def dot(a, b):
    return jnp.dot(a, b, preferred_element_type=F32)


def silu(v):
    return v + v * jnp.tanh(v)


def column(row):
    return jnp.transpose(jnp.broadcast_to(row, (128, row.shape[1])))


def store_weights(w_ref, stack_ref, low_ref):
    for b in range(w_ref.shape[0] // 128):
        hi, lo = split(0.5 * w_ref[128 * b : 128 * (b + 1), :])
        stack_ref[256 * b : 256 * b + 128, :] = hi
        stack_ref[256 * b + 128 : 256 * b + 256, :] = hi
        low_ref[128 * b : 128 * (b + 1), :] = lo


def store_out_weights(w_ref, pair_ref):
    hi, lo = split(w_ref[...])
    pair_ref[:, :128] = hi
    pair_ref[:, 128:] = lo


def out_layer(hidden, pair_ref):
    hi, lo = split(hidden)
    both = dot(hi, pair_ref[...])
    return both[:, :128] + both[:, 128:] + dot(lo, pair_ref[:, :128])


def kernel(
    sizes,
    node_h, hub_h, edge_h, src_h, dst_h, sgn_h, rows_h, w1_h, b1_h, w2_h, b2_h, w3_h, b3_h, w4_h, b4_h,
    node_out, hub_out,
    node, hub, edge, src, dst, sgn, rows, w1, b1, w2, b2, w3, b3, w4, b4, in_sem,
    w1s, w1l, w2p, w3s, w3l, w4p,
    table, outbuf, mir, hubs, own_s, own_d, oh_s, oh_d, x_s, x_d, oh_t, sums, dacc, msg, got_msg, hubb, hubsend,
    m_send, m_recv, h_send, h_recv, r_send, r_recv, a_send, a_recv, g_send, g_recv,
):
    L, G, V, CAP, H, HS, E, EB, T, TP = sizes
    LC = L * CAP
    lane = lax.axis_index("lane")
    group = lax.axis_index("group")
    barrier = pltpu.get_barrier_semaphore()
    lanes = [lax.rem(lane + k, L) for k in range(1, L)]
    groups = [lax.rem(group + k, G) for k in range(1, G)]
    for p in lanes:
        pl.semaphore_signal(barrier, inc=1, device_id=(group, p), device_id_type=MESH)
    for q in groups:
        pl.semaphore_signal(barrier, inc=1, device_id=(q, lane), device_id_type=MESH)

    far = (rows_h, node_h, hub_h, src_h, dst_h, w1_h, edge_h, w2_h, sgn_h, b1_h, b2_h, w3_h, w4_h, b3_h, b4_h)
    near = (rows, node, hub, src, dst, w1, edge, w2, sgn, b1, b2, w3, w4, b3, b4)
    loads = [pltpu.make_async_copy(f, n, in_sem.at[i]) for i, (f, n) in enumerate(zip(far, near))]
    for c in loads:
        c.start()
    for c in loads[:3]:
        c.wait()

    hi, lo = split(node[...])
    table[:V, :128] = hi
    table[:V, 128:] = lo
    if TP > T:
        table[T:, :] = jnp.zeros((TP - T, 256), BF16)
    LCP = -(-LC // 128) * 128
    pieces = [rows[p : p + 1, :] for p in range(L)]
    if LCP > LC:
        pieces.append(jnp.full((1, LCP - LC), -1, jnp.int32))
    flat_rows = jnp.concatenate(pieces, axis=1)
    lane_iota = lax.broadcasted_iota(jnp.int32, (128, 128), 1)
    flat_col = column(flat_rows)[:LC]
    lane_iota_lc = lax.broadcasted_iota(jnp.int32, (LC, 128), 1)
    send_hot = jnp.concatenate(
        [jnp.where(flat_col == lane_iota_lc + 128 * k, 1.0, 0.0).astype(BF16) for k in range(V // 128)], axis=1
    )
    both = dot(send_hot, table[:V, :])
    outbuf[...] = both[:, :128] + both[:, 128:]

    pl.semaphore_wait(barrier, L - 1 + G - 1)

    def remote(src_ref, dst_ref, s_sem, r_sem, g, l):
        return pltpu.make_async_remote_copy(
            src_ref=src_ref, dst_ref=dst_ref, send_sem=s_sem, recv_sem=r_sem,
            device_id=(g, l), device_id_type=MESH,
        )

    def part(p, n, start=0):
        return pl.ds(pl.multiple_of(start + p * n, 16), n)

    sends = []
    for p in lanes:
        c = remote(outbuf.at[part(p, CAP)], mir.at[part(lane, CAP)], m_send.at[p], m_recv.at[lane], group, p)
        c.start()
        sends.append(c)
        c = remote(hub, hubs.at[part(lane, HS)], h_send.at[p], h_recv.at[lane], group, p)
        c.start()
        sends.append(c)
    mir[part(lane, CAP), :] = outbuf[part(lane, CAP), :]
    hubs[part(lane, HS), :] = hub[...]

    for c in loads[3:5]:
        c.wait()
    NR = EB // 128
    lane_id = lane_iota.astype(F32).astype(BF16)
    sub_id = lax.broadcasted_iota(jnp.int32, (128, 128), 0).astype(F32).astype(BF16)
    one, zero = jnp.ones((128, 128), BF16), jnp.zeros((128, 128), BF16)

    def digits(ids):
        high = ids >> 7
        return (ids & 127).astype(F32).astype(BF16), high.astype(F32).astype(BF16)

    def own_block(i, carry):
        for ids, own, other, found in ((src, own_s, oh_s, x_s), (dst, own_d, oh_d, x_d)):
            for j in range(NR):
                low, high = digits(column(ids[pl.ds(i * NR + j, 1), :]))
                hot = jnp.where(low == lane_id, one, zero)
                for k in range(TP // 128):
                    place = jnp.where(high == jnp.asarray(k, BF16), hot, zero)
                    if 128 * k < V:
                        own[128 * j : 128 * (j + 1), 128 * k : 128 * (k + 1)] = place
                    else:
                        other[part(i * NR + j, 128), 128 * k - V : 128 * (k + 1) - V] = place
            found[part(i, EB), :] = dot(own[...], table[:V, :]).astype(BF16)
        return carry

    lax.fori_loop(0, E // EB, own_block, 0)

    for c in loads[5:]:
        c.wait()
    store_weights(w1, w1s, w1l)
    store_out_weights(w2, w2p)
    store_weights(w3, w3s, w3l)
    store_out_weights(w4, w4p)
    sums[...] = jnp.zeros(sums.shape, F32)
    dacc[...] = jnp.zeros(dacc.shape, BF16)

    for p in lanes:
        remote(outbuf.at[part(p, CAP)], mir.at[part(p, CAP)], m_send.at[p], m_recv.at[p], group, p).wait_recv()
        remote(hub, hubs.at[part(p, HS)], h_send.at[p], h_recv.at[p], group, p).wait_recv()
    hi, lo = split(mir[...])
    table[V : V + LC, :128] = hi
    table[V : V + LC, 128:] = lo
    hi, lo = split(hubs[...])
    table[V + LC : T, :128] = hi
    table[V + LC : T, 128:] = lo

    def edge_block(i, carry):
        signs = []
        for j in range(NR):
            at = pl.ds(i * NR + j, 1)
            row = slice(128 * j, 128 * (j + 1))
            r_low, r_high = digits(jnp.broadcast_to(dst[at, :], (128, 128)))
            r_hot = jnp.where(r_low == sub_id, one, zero)
            for k in range(TP // 128):
                n = min(128, T - 128 * k)
                hot = jnp.where(r_high == jnp.asarray(k, BF16), r_hot, zero)[:n]
                oh_t[128 * k : 128 * k + n, row] = hot
                dacc[128 * k : 128 * k + n, :] += hot
            signs.append((2 * column(sgn[at, :]) - 1).astype(F32))
        here = part(i, EB)
        xs = (x_s[here, :].astype(F32) + dot(oh_s[here, :], table[V:, :])).astype(BF16)
        xd = (x_d[here, :].astype(F32) + dot(oh_d[here, :], table[V:, :])).astype(BF16)
        eh, el = split(edge[pl.ds(pl.multiple_of(i * EB, EB), EB), :])
        pre = dot(jnp.concatenate([xs, xd, eh, el], axis=1), w1s[...])
        pre = pre + dot(jnp.concatenate([xs[:, :128], xd[:, :128], eh], axis=1), w1l[...])
        h = silu(pre + 0.5 * b1[...])
        m = (out_layer(h, w2p) + b2[...]) * jnp.concatenate(signs, axis=0)
        mh, ml = split(m)
        sums[...] += dot(oh_t[...], jnp.concatenate([mh, ml], axis=1))
        return carry

    lax.fori_loop(0, E // EB, edge_block, 0)

    for p in range(L):
        hub_at, mir_at = V + LC + p * HS, V + p * CAP
        msg[p, :HS] = sums[hub_at : hub_at + HS, :128] + sums[hub_at : hub_at + HS, 128:]
        counts = jnp.concatenate(
            [dacc[hub_at : hub_at + HS, :], dacc[mir_at : mir_at + CAP, :], zero[: 128 - HS - CAP]], axis=0
        )
        msg[p, HS : HS + 8] = lax.dot_general(
            one[:8], counts, (((1,), (1,)), ((), ())), preferred_element_type=F32
        )
    first, second = pl.ds(0, HS + 8), pl.ds(HS + 8, CAP)
    for p in lanes:
        c = remote(msg.at[p, first], got_msg.at[lane, first], a_send.at[p], a_recv.at[lane], group, p)
        c.start()
        sends.append(c)
    for p in range(L):
        mir_at = V + p * CAP
        msg[p, HS + 8 :] = sums[mir_at : mir_at + CAP, :128] + sums[mir_at : mir_at + CAP, 128:]
    for p in lanes:
        c = remote(msg.at[p, second], got_msg.at[lane, second], r_send.at[p], r_recv.at[lane], group, p)
        c.start()
        sends.append(c)
    got_msg[lane] = msg[lane]

    def own_part(x):
        return dot(jnp.concatenate(split(x), axis=1), w3s[:256]) + dot(x.astype(BF16), w3l[:128]) + 0.5 * b3[...]

    node_pre = own_part(node[...])
    hub_pre = own_part(hub[...])
    own_sum = sums[:V, :128] + sums[:V, 128:]
    own_deg = dot(dacc[:V, :], one)
    v_iota = lax.broadcasted_iota(jnp.int32, (V, LC), 0)
    back_hot = jnp.where(v_iota == flat_rows[:, :LC], 1.0, 0.0).astype(BF16)

    for p in lanes:
        remote(msg.at[p, first], got_msg.at[p, first], a_send.at[p], a_recv.at[p], group, p).wait_recv()
    total = got_msg[0, : HS + 8]
    for p in range(1, L):
        total = total + got_msg[p, : HS + 8]
    hubsend[...] = total
    for q in groups:
        c = remote(hubsend, hubb.at[group], g_send.at[q], g_recv.at[group], q, lane)
        c.start()
        sends.append(c)
    hubb[group] = hubsend[...]

    for p in lanes:
        remote(msg.at[p, second], got_msg.at[p, second], r_send.at[p], r_recv.at[p], group, p).wait_recv()
    sh, sl = split(jnp.concatenate([got_msg[p, HS + 8 :] for p in range(L)], axis=0))
    dh, dl = split(
        jnp.concatenate([column(got_msg[p, HS : HS + 1])[HS : HS + CAP] for p in range(L)], axis=0)
    )
    got = dot(back_hot, jnp.concatenate([sh, sl], axis=1))
    got_deg = dot(back_hot, jnp.concatenate([dh, dl], axis=1))

    def update(x, pre, summed, degree):
        mh, ml = split(summed / jnp.maximum(degree, 1.0))
        pre = pre + dot(jnp.concatenate([mh, ml], axis=1), w3s[256:]) + dot(mh, w3l[128:])
        return x + out_layer(silu(pre), w4p) + b4[...]

    node_out[...] = update(
        node[...],
        node_pre,
        own_sum + got[:, :128] + got[:, 128:],
        own_deg + got_deg[:, :128] + got_deg[:, 128:],
    )

    for q in groups:
        remote(hubsend, hubb.at[q], g_send.at[q], g_recv.at[q], q, lane).wait_recv()
    whole = hubb[0]
    for q in range(1, G):
        whole = whole + hubb[q]
    hub_out[...] = update(hub[...], hub_pre, whole[:HS, :], column(whole[HS : HS + 1, :])[:HS])
    for c in sends:
        c.wait_send()


def per_device(node, hub, edge, src, dst, sgn, rows, w1, b1, w2, b2, w3, b3, w4, b4):
    L, G = lax.axis_size("lane"), lax.axis_size("group")
    V, D = node.shape
    CAP = rows.shape[1]
    HS = hub.shape[0]
    H = HS * L
    E = edge.shape[0]
    HID = w1.shape[1]
    EB = math.gcd(512, E)
    T = V + L * CAP + H
    TP = -(-T // 128) * 128
    sizes = (L, G, V, CAP, H, HS, E, EB, T, TP)
    assert E <= 256 * 128 and HS + CAP <= 128 and V % 128 == 0
    dma = pltpu.SemaphoreType.DMA
    vmem = pl.BlockSpec(memory_space=pltpu.VMEM)
    args = (
        node, hub, edge, src.reshape(-1, 128), dst.reshape(-1, 128), sgn.reshape(-1, 128), rows,
        w1, b1.reshape(1, -1), w2, b2.reshape(1, -1), w3, b3.reshape(1, -1), w4, b4.reshape(1, -1),
    )
    return pl.pallas_call(
        functools.partial(kernel, sizes),
        out_shape=(pltpu.VMEM((V, D), F32), pltpu.VMEM((HS, D), F32)),
        in_specs=[pl.BlockSpec(memory_space=pltpu.HBM)] * 15,
        out_specs=(vmem, vmem),
        scratch_shapes=[pltpu.VMEM(a.shape, a.dtype) for a in args]
        + [dma((15,))]
        + [
            pltpu.VMEM((6 * D, HID), BF16),
            pltpu.VMEM((3 * D, HID), BF16),
            pltpu.VMEM((HID, 2 * D), BF16),
            pltpu.VMEM((4 * D, HID), BF16),
            pltpu.VMEM((2 * D, HID), BF16),
            pltpu.VMEM((HID, 2 * D), BF16),
            pltpu.VMEM((TP, 2 * D), BF16),
            pltpu.VMEM((L * CAP, D), F32),
            pltpu.VMEM((L * CAP, D), F32),
            pltpu.VMEM((H, D), F32),
            pltpu.VMEM((EB, V), BF16),
            pltpu.VMEM((EB, V), BF16),
            pltpu.VMEM((E, TP - V), BF16),
            pltpu.VMEM((E, TP - V), BF16),
            pltpu.VMEM((E, 2 * D), BF16),
            pltpu.VMEM((E, 2 * D), BF16),
            pltpu.VMEM((T, EB), BF16),
            pltpu.VMEM((T, 2 * D), F32),
            pltpu.VMEM((T, 128), BF16),
            pltpu.VMEM((L, HS + 8 + CAP, D), F32),
            pltpu.VMEM((L, HS + 8 + CAP, D), F32),
            pltpu.VMEM((G, HS + 8, D), F32),
            pltpu.VMEM((HS + 8, D), F32),
        ]
        + [dma((L,))] * 8
        + [dma((G,))] * 2,
        compiler_params=pltpu.CompilerParams(
            collective_id=0, has_side_effects=True, vmem_limit_bytes=63 * 2**20
        ),
    )(*args)


def solution(mesh):
    rows = P(("group", "lane"), None)
    flat = P(("group", "lane"))
    return jax.shard_map(
        per_device,
        mesh=mesh,
        in_specs=(rows, P("lane", None), rows, flat, flat, flat, rows) + (P(),) * 8,
        out_specs=(rows, P("lane", None)),
        check_vma=False,
    )
```
